128 devices in a mesh: band: 8 (over z_hi, x), gvec: 16 (over y, z_lo, core).
Axes of the slice: x: 4, y: 4, z: 4 (z_hi: 2, z_lo: 2; z = z_hi * 2 + z_lo), core: 2. Of those that a mesh axis runs over, the one named last changes fastest.
Arguments:
- coeffs: bfloat16 [131072, 1024], P('gvec', 'band'), may hold values from -6 to 6
- rotation: bfloat16 [1024, 4096], P('gvec', 'band'), may hold values from -0.1875 to 0.1875
Outputs:
- rotated: bfloat16 [131072, 4096], P('gvec', 'band')
The draws below stay inside these ranges and needn't reach their ends.
All inputs are finite; a program needn't handle non-finite values.
Results may differ from the reference program's by a relative error of at most 0.001.
Values may be sent and summed in bfloat16 or wider, within the bound.
A program may use at most 128 MiB of HBM per device.

```python
import jax
import jax.numpy as jnp

NB = 4096
KW = 1024
NG = 131072


def block_levels(key, shape, shards, low, high):
    def one(axis_at, shards_of):
        steps = jax.random.uniform(jax.random.fold_in(jax.random.fold_in(key, 6), axis_at), (shards_of,), jnp.float32, low / len(shards), high / len(shards))
        return jnp.repeat(jnp.exp(steps), shape[axis_at] // shards_of).reshape((-1,) + (1,) * (len(shape) - axis_at - 1))

    loudness = one(*shards[0])
    for cut in shards[1:]:
        loudness = loudness * one(*cut)
    return loudness


def normal_values(key, shape, deviation, reach, pieces=(), dtype=jnp.bfloat16):
    result = jax.random.normal(key, shape, jnp.float32) * deviation
    if len(pieces) > 0:
        result = block_levels(key, shape, pieces, -0.22, 0.18) * result
    return jnp.clip(result, min=-reach, max=reach).astype(dtype)


def setup_inputs(seed: int = 0) -> dict:
    keys = jax.random.split(jax.random.key(seed), 3)
    coeffs = normal_values(keys[0], (NG, KW), 1.0, 6.0, ((0, 16), (1, 8)))
    rotation = normal_values(keys[1], (KW, NB), KW ** -0.5, 0.1875, ((0, 16), (1, 8)))
    return dict(coeffs=coeffs, rotation=rotation)


def reference(coeffs, rotation):
    product = jnp.dot(coeffs, rotation, preferred_element_type=jnp.float32)
    return product.astype(jnp.bfloat16)
```

```python
import functools

import jax
import jax.numpy as jnp
from jax import lax
from jax.experimental import pallas as pl
from jax.experimental.pallas import tpu as pltpu
from jax.sharding import PartitionSpec as P

MESH = pl.DeviceIdType.MESH
R = 256
AHEAD = 2
START = 4


def kernel(nb, n, coef, rot, out, gath, full, prod, *sems):
    (own_s, own_r, par_s, par_r, fwd_s, fwd_r, k_s, k_r, p_s, p_r, z_s, z_r, y_s, y_r, c_s, c_r, loc) = sems
    half = R // 2
    band, gvec = lax.axis_index("band"), lax.axis_index("gvec")
    x, zh = lax.rem(band, 4), band // 4
    y, zl, c = gvec // 4, lax.rem(gvec // 2, 2), lax.rem(gvec, 2)
    xp, xm = lax.rem(x + 1, 4), lax.rem(x + 3, 4)
    oh = 1 - zh

    def at(x_=x, y_=y, zh_=zh, zl_=zl, c_=c):
        return (zh_ * 4 + x_, y_ * 4 + zl_ * 2 + c_)

    right, left, across = at(x_=xp), at(x_=xm), at(zh_=oh)
    z_peers = (at(zl_=1 - zl), at(zh_=oh, zl_=1 - zl), across)
    y_peers = tuple(at(y_=lax.rem(y + d, 4)) for d in (1, 3, 2))
    twin = at(c_=1 - c)

    def send(src, dst, s, r, dev):
        return pltpu.make_async_remote_copy(src_ref=src, dst_ref=dst, send_sem=s, recv_sem=r, device_id=dev, device_id_type=MESH)

    def row(i, plane):
        return pl.multiple_of(jnp.where(i < nb, plane * nb + i, nb + i) * R, R)

    def own(i, d):
        rows = pl.ds(row(i, zh), R)
        return send(coef.at[rows], gath.at[x, zh, rows], own_s.at[d, i], own_r.at[d, i], (right, left)[d])

    def partner(i, d):
        ref = gath.at[x, oh, pl.ds(row(i, zh), R)]
        return send(ref, ref, par_s.at[d, i], par_r.at[d, i], (right, left)[d])

    def forward(i, d):
        ref = gath.at[(xm, xp)[d], :, pl.ds(row(i, zh) + d * half, half)]
        return send(ref, ref, fwd_s.at[d, i], fwd_r.at[d, i], (right, left)[d])

    def over(i):
        rows = pl.ds(row(i, oh), R)
        return send(coef.at[rows], gath.at[x, zh, rows], k_s.at[i], k_r.at[i], across)

    def product(i):
        return send(prod.at[pl.ds(i * R, R)], out.at[pl.ds(row(i, zh), R)], p_s.at[i], p_r.at[i], across)

    def compute(i):
        for d in range(2):
            forward(i, d).wait_recv()
        rows = pl.ds(row(i, zh), R)

        def times(columns):
            lhs = jnp.concatenate([gath[b % 4, b // 4, rows, :] for b in range(8)], axis=1)
            rhs = full[columns].reshape(1024, full.shape[-1])
            return jnp.dot(lhs, rhs, preferred_element_type=jnp.float32).astype(out.dtype)

        @pl.when(i < nb)
        def _():
            prod[pl.ds(i * R, R), :] = times(oh)
            product(i).start()

        out[rows, :] = times(zh)

    mine = full.at[zh, y, zl, c]
    z_sends = [send(rot, mine, z_s.at[k], z_r.at[k], dev) for k, dev in enumerate(z_peers)]
    line = full.at[:, y, :, c]
    y_sends = [send(line, line, y_s.at[k], y_r.at[k], dev) for k, dev in enumerate(y_peers)]
    plane = full.at[:, :, :, c]
    c_send = send(plane, plane, c_s, c_r, twin)

    local_rot = pltpu.make_async_copy(rot, mine, loc.at[0])
    local_coef = pltpu.make_async_copy(coef, gath.at[x, zh], loc.at[1])

    peers = (right, left, *z_peers, *y_peers, twin)
    barrier = pltpu.get_barrier_semaphore()
    for dev in peers:
        pl.semaphore_signal(barrier, inc=1, device_id=dev, device_id_type=MESH)
    local_rot.start()
    pl.semaphore_wait(barrier, len(peers))

    over(0).start()
    for i in range(AHEAD):
        for d in range(2):
            own(i, d).start()
    for s in z_sends:
        s.start()

    @pl.loop(1, n)
    def _(i):
        over(i).start()

    local_coef.start()
    local_rot.wait()
    local_coef.wait()

    def begin(t):
        return jnp.maximum(0, jnp.minimum(2 * (t - START), t - 2))

    @pl.loop(0, n + 2)
    def _(t):
        @pl.when(t + AHEAD < n)
        def _():
            for d in range(2):
                own(t + AHEAD, d).start()

        @pl.when(t < n)
        def _():
            over(t).wait_recv()
            for d in range(2):
                partner(t, d).start()

        @pl.when(jnp.logical_and(t >= 1, t < n + 1))
        def _():
            for d in range(2):
                own(t - 1, d).wait_recv()
                partner(t - 1, d).wait_recv()
                forward(t - 1, d).start()

        @pl.when(t == 1)
        def _():
            for s in z_sends:
                s.wait()
            for s in y_sends:
                s.start()

        @pl.when(t == START - 1)
        def _():
            for s in y_sends:
                s.wait()
            c_send.start()

        @pl.when(t == START)
        def _():
            c_send.wait()

        @pl.loop(begin(t), begin(t + 1))
        def _(i):
            compute(i)

    @pl.loop(0, nb)
    def _(i):
        product(i).wait()

    @pl.loop(0, n)
    def _(i):
        over(i).wait_send()
        for d in range(2):
            own(i, d).wait_send()
            partner(i, d).wait_send()
            forward(i, d).wait_send()


def on_device(coeffs, rotation):
    rows, depth = coeffs.shape
    columns = rotation.shape[1]
    nb = rows // R // 3
    n = rows // R - nb
    dma = pltpu.SemaphoreType.DMA
    return pl.pallas_call(
        functools.partial(kernel, nb, n),
        out_shape=jax.ShapeDtypeStruct((rows, columns), coeffs.dtype),
        in_specs=[pl.BlockSpec(memory_space=pl.ANY)] * 2,
        out_specs=pl.BlockSpec(memory_space=pltpu.VMEM),
        scratch_shapes=[
            pltpu.VMEM((4, 2, rows, depth), coeffs.dtype),
            pltpu.VMEM((2, 4, 2, 2, rotation.shape[0], columns), coeffs.dtype),
            pltpu.VMEM((nb * R, columns), coeffs.dtype),
            dma((2, n)), dma((2, n)), dma((2, n)), dma((2, n)), dma((2, n)), dma((2, n)),
            dma((n,)), dma((n,)), dma((nb,)), dma((nb,)),
            dma((3,)), dma((3,)), dma((3,)), dma((3,)), dma, dma, dma((2,)),
        ],
        compiler_params=pltpu.CompilerParams(
            collective_id=0, has_side_effects=True, vmem_limit_bytes=56 * 2**20
        ),
        cost_estimate=pl.CostEstimate(flops=2 * rows * 1024 * columns, bytes_accessed=rows * columns * 2, transcendentals=0),
    )(coeffs, rotation)


def solution(mesh):
    return jax.shard_map(
        on_device,
        mesh=mesh,
        in_specs=(P("gvec", "band"), P("gvec", "band")),
        out_specs=P("gvec", "band"),
        check_vma=False,
    )
```

```python
import functools

import jax
import jax.numpy as jnp
from jax import lax
from jax.experimental import pallas as pl
from jax.experimental.pallas import tpu as pltpu
from jax.sharding import PartitionSpec as P

MESH = pl.DeviceIdType.MESH
R = 128
NJ = 7
K_AHEAD, OWN_AHEAD = 6, 4
L_PARTNER, L_FORWARD, L_MULTIPLY = 3, 6, 9
FIRST_MATE, FIRST_PAIR = 6, 11
ROT_1, ROT_2, ROT_3, START, ROT_4, ROT_5 = 2, 4, 6, 7, 9, 10


def kernel(nb, nj, coef, rot, out, gath, full, prod, jprod, *sems):
    (own_s, own_r, par_s, par_r, fwd_s, fwd_r, k_s, k_r, p_s, p_r,
     feed_s, feed_r, jk_s, jk_r, jf_s, jf_r, ma_s, ma_r, mb_s, mb_r, jo_s, jo_r,
     z_s, z_r, x_s, x_r, y_s, y_r, c_s, c_r, loc) = sems
    half = R // 2
    band, gvec = lax.axis_index("band"), lax.axis_index("gvec")
    x, zh = lax.rem(band, 4), band // 4
    y, zl, c = gvec // 4, lax.rem(gvec // 2, 2), lax.rem(gvec, 2)
    xp, xm, x2 = lax.rem(x + 1, 4), lax.rem(x + 3, 4), lax.rem(x + 2, 4)
    oh = 1 - zh

    def at(x_=x, y_=y, zh_=zh, zl_=zl, c_=c):
        return (zh_ * 4 + x_, y_ * 4 + zl_ * 2 + c_)

    right, left, across = at(x_=xp), at(x_=xm), at(zh_=oh)
    ways = (right, left)
    z_peers = (at(zl_=1 - zl), across, at(zh_=oh, zl_=1 - zl))
    y_peers = tuple(at(y_=lax.rem(y + d, 4)) for d in (1, 3, 2))
    twin = at(c_=1 - c)

    def send(src, dst, s, r, dev):
        return pltpu.make_async_remote_copy(src_ref=src, dst_ref=dst, send_sem=s, recv_sem=r, device_id=dev, device_id_type=MESH)


    def rows_of(i, plane):
        return pl.ds(pl.multiple_of((plane * nb + i) * R, R), R)

    def own(i, d):
        rows = rows_of(i, zh)
        return send(coef.at[rows], gath.at[x, zh, rows], own_s.at[d], own_r.at[d, i], ways[d])

    def partner(i, d):
        ref = gath.at[x, oh, rows_of(i, zh)]
        return send(ref, ref, par_s.at[d], par_r.at[d, i], ways[d])

    def forward(i, d):
        ref = gath.at[(xm, xp)[d], :, pl.ds(pl.multiple_of((zh * nb + i) * R + d * half, half), half)]
        return send(ref, ref, fwd_s.at[d], fwd_r.at[d, i], ways[d])

    def over(i):
        rows = rows_of(i, oh)
        return send(coef.at[rows], gath.at[x, zh, rows], k_s, k_r.at[i], across)

    def product(i):
        return send(prod.at[pl.ds(i * R, R)], out.at[rows_of(i, zh)], p_s, p_r, across)


    pair = (x, xm)
    feeder = (xm, xp)
    fed = (xp, x2)

    def pair_rows(i, j):
        return pl.ds(pl.multiple_of((2 * nb + j * nj + i) * R, R), R)

    def feed(i, d):
        rows = pair_rows(i, fed[d])
        return send(coef.at[rows], gath.at[x, zh, rows], feed_s.at[d], feed_r.at[d, i], ways[d])

    def pair_over(i, d):
        rows = pair_rows(i, pair[d])
        return send(coef.at[rows], gath.at[x, zh, rows], jk_s.at[d], jk_r.at[d, i], across)

    def feeder_over(i, d):
        ref = gath.at[feeder[d], zh, pair_rows(i, pair[d])]
        return send(ref, ref, jf_s.at[d], jf_r.at[d, i], across)

    def mate_own(i, d):
        ref = gath.at[x, :, pair_rows(i, pair[d])]
        return send(ref, ref, ma_s.at[d], ma_r.at[d, i], ways[d])

    def mate_fed(i, d):
        ref = gath.at[feeder[d], :, pair_rows(i, pair[d])]
        return send(ref, ref, mb_s.at[d], mb_r.at[d, i], ways[d])

    def pair_product(i, d):
        return send(jprod.at[d, pl.ds(i * R, R)], out.at[pair_rows(i, pair[d])], jo_s.at[d], jo_r.at[d], ways[1 - d])


    z_sends = [send(rot, full.at[(0, 1, 1)[k], y, zl, c], z_s.at[k], z_r.at[k], dev) for k, dev in enumerate(z_peers)]
    x_sends = [send(full.at[0, y, :, c], full.at[2 + d, y, :, c], x_s.at[d], x_r.at[d], ways[d]) for d in range(2)]

    def y_sends(g):
        ref = full.at[2 * g : 2 * g + 2, y, :, c]
        return [send(ref, ref, y_s.at[g, k], y_r.at[g, k], dev) for k, dev in enumerate(y_peers)]

    def c_send(g):
        ref = full.at[2 * g : 2 * g + 2, :, :, c]
        return send(ref, ref, c_s.at[g], c_r.at[g], twin)

    def times(rows, columns):
        lhs = jnp.concatenate([gath[b % 4, b // 4, rows, :] for b in range(8)], axis=1)
        rhs = full[columns].reshape(1024, full.shape[-1])
        return jnp.dot(lhs, rhs, preferred_element_type=jnp.float32).astype(out.dtype)

    local_rot = pltpu.make_async_copy(rot, full.at[0, y, zl, c], loc.at[0])
    local_coef = pltpu.make_async_copy(coef, gath.at[x, zh], loc.at[1])

    peers = (right, left, *z_peers, *y_peers, twin)
    barrier = pltpu.get_barrier_semaphore()
    for dev in peers:
        pl.semaphore_signal(barrier, inc=1, device_id=dev, device_id_type=MESH)
    local_rot.start()
    pl.semaphore_wait(barrier, len(peers))

    over(0).start()
    for i in range(OWN_AHEAD):
        for d in range(2):
            own(i, d).start()
    for s in z_sends:
        s.start()
    for i in range(1, K_AHEAD):
        over(i).start()
    local_coef.start()
    local_rot.wait()
    local_coef.wait()

    def begin(t):
        return jnp.maximum(0, jnp.minimum(jnp.minimum(2 * (t - START), t - L_MULTIPLY), nb))

    def between(t, first, count, step=1):
        inside = jnp.logical_and(t >= first, t < first + step * count)
        return inside if step == 1 else jnp.logical_and(inside, lax.rem(t - first + step, step) == 0)

    steps = max(nb + L_MULTIPLY, FIRST_PAIR + 2 * nj - 1)

    @pl.loop(0, steps)
    def _(t):
        @pl.when(between(t, OWN_AHEAD, nb - OWN_AHEAD))
        def _():
            for d in range(2):
                own(t, d).start()

        @pl.when(between(t, 0, nb - K_AHEAD))
        def _():
            over(t + K_AHEAD).start()

        @pl.when(between(t, 0, nj))
        def _():
            for d in range(2):
                feed(t, d).start()
                pair_over(t, d).start()

        @pl.when(between(t, L_PARTNER, nb))
        def _():
            over(t - L_PARTNER).wait_recv()
            for d in range(2):
                partner(t - L_PARTNER, d).start()

        @pl.when(between(t, 2, nj))
        def _():
            for d in range(2):
                feed(t - 2, d).wait_recv()
                feeder_over(t - 2, d).start()

        @pl.when(between(t, L_FORWARD, nb))
        def _():
            for d in range(2):
                own(t - L_FORWARD, d).wait_recv()
                partner(t - L_FORWARD, d).wait_recv()
                forward(t - L_FORWARD, d).start()

        @pl.when(between(t, FIRST_MATE, nj, 2))
        def _():
            i = (t - FIRST_MATE) // 2
            for d in range(2):
                pair_over(i, d).wait_recv()
                mate_own(i, d).start()
            for d in range(2):
                feeder_over(i, d).wait_recv()
                mate_fed(i, d).start()

        @pl.when(t == ROT_1)
        def _():
            for s in z_sends:
                s.wait()
            for s in x_sends:
                s.start()
            for s in y_sends(0):
                s.start()

        @pl.when(t == ROT_2)
        def _():
            for s in x_sends:
                s.wait()
            for s in y_sends(1):
                s.start()

        @pl.when(t == ROT_3)
        def _():
            for s in y_sends(0):
                s.wait()
            c_send(0).start()

        @pl.when(t == START)
        def _():
            c_send(0).wait()

        @pl.when(t == ROT_4)
        def _():
            for s in y_sends(1):
                s.wait()
            c_send(1).start()

        @pl.when(t == ROT_5)
        def _():
            c_send(1).wait()

        @pl.loop(begin(t), begin(t + 1))
        def _(i):
            for d in range(2):
                forward(i, d).wait_recv()
            rows = rows_of(i, zh)
            prod[pl.ds(i * R, R), :] = times(rows, 1)
            product(i).start()
            out[rows, :] = times(rows, 0)

        @pl.when(between(t, FIRST_PAIR, nj, 2))
        def _():
            i = (t - FIRST_PAIR) // 2
            for d in range(2):
                mate_own(i, 1 - d).wait_recv()
                mate_fed(i, 1 - d).wait_recv()
                rows = pair_rows(i, pair[d])
                jprod[d, pl.ds(i * R, R), :] = times(rows, 2 + d)
                pair_product(i, d).start()
            for d in range(2):
                rows = pair_rows(i, pair[d])
                out[rows, :] = times(rows, 0)


    send(prod, prod, p_s, p_r, across).wait()
    for d in range(2):
        send(jprod.at[d], jprod.at[d], jo_s.at[d], jo_r.at[d], ways[d]).wait()

    def sent(s, blocks):
        ref = gath.at[0, 0, pl.ds(0, blocks * R)]
        send(ref, ref, s, p_r, across).wait_send()

    sent(k_s, nb)
    for d in range(2):
        for s in (own_s, par_s, fwd_s):
            sent(s.at[d], nb)
        for s in (feed_s, jk_s, jf_s):
            sent(s.at[d], nj)
        for s in (ma_s, mb_s):
            sent(s.at[d], 2 * nj)


def on_device(coeffs, rotation):
    coeffs, rotation = (pltpu.with_memory_space_constraint(v, pltpu.HBM) for v in (coeffs, rotation))
    rows, depth = coeffs.shape
    columns = rotation.shape[1]
    nj = NJ
    nb = (rows // R - 4 * nj) // 2
    dma = pltpu.SemaphoreType.DMA
    dtype = coeffs.dtype
    return pl.pallas_call(
        functools.partial(kernel, nb, nj),
        out_shape=pltpu.VMEM((rows, columns), dtype),
        in_specs=[pl.BlockSpec(memory_space=pltpu.HBM)] * 2,
        out_specs=pl.BlockSpec(memory_space=pltpu.VMEM),
        scratch_shapes=[
            pltpu.VMEM((4, 2, rows, depth), dtype),
            pltpu.VMEM((4, 4, 2, 2, rotation.shape[0], columns), dtype),
            pltpu.VMEM((nb * R, columns), dtype),
            pltpu.VMEM((2, nj * R, columns), dtype),
            dma((2,)), dma((2, nb)), dma((2,)), dma((2, nb)), dma((2,)), dma((2, nb)), dma, dma((nb,)), dma, dma,
            dma((2,)), dma((2, nj)), dma((2,)), dma((2, nj)), dma((2,)), dma((2, nj)),
            dma((2,)), dma((2, nj)), dma((2,)), dma((2, nj)), dma((2,)), dma((2,)),
            dma((3,)), dma((3,)), dma((2,)), dma((2,)), dma((2, 3)), dma((2, 3)), dma((2,)), dma((2,)), dma((2,)),
        ],
        compiler_params=pltpu.CompilerParams(
            collective_id=0, has_side_effects=True, vmem_limit_bytes=40 * 2**20
        ),
        cost_estimate=pl.CostEstimate(flops=2 * rows * 1024 * columns, bytes_accessed=rows * columns * 2, transcendentals=0),
    )(coeffs, rotation)


def solution(mesh):
    return jax.shard_map(
        on_device,
        mesh=mesh,
        in_specs=(P("gvec", "band"), P("gvec", "band")),
        out_specs=P("gvec", "band"),
        check_vma=False,
    )
```

```python
import functools

import jax
import jax.numpy as jnp
from jax import lax
from jax.experimental import pallas as pl
from jax.experimental.pallas import tpu as pltpu
from jax.sharding import PartitionSpec as P

MESH = pl.DeviceIdType.MESH
R = 128
NJ = 7
K_AHEAD, OWN_AHEAD = 11, 5
L_PARTNER, L_FORWARD, L_MULTIPLY = 0, 5, 9
L_FEED, FIRST_MATE, FIRST_PAIR, STRIDE = 2, 6, 14, 3
ROT_1, ROT_2, ROT_3, START, ROT_4, ROT_5 = 1, 3, 6, 11, 12, 14


def kernel(nb, nj, coef, rot, out, gath, full, prod, jprod, *sems):
    (own_s, own_r, par_s, par_r, fwd_s, fwd_r, k_s, k_r, p_s, p_r,
     feed_s, feed_r, jk_s, jk_r, jf_s, jf_r, ma_s, ma_r, mb_s, mb_r, jo_s, jo_r,
     z_s, z_r, x_s, x_r, y_s, y_r, c_s, c_r, loc) = sems
    half = R // 2
    band, gvec = lax.axis_index("band"), lax.axis_index("gvec")
    x, zh = lax.rem(band, 4), band // 4
    y, zl, c = gvec // 4, lax.rem(gvec // 2, 2), lax.rem(gvec, 2)
    xp, xm, x2 = lax.rem(x + 1, 4), lax.rem(x + 3, 4), lax.rem(x + 2, 4)
    oh = 1 - zh

    def at(x_=x, y_=y, zh_=zh, zl_=zl, c_=c):
        return (zh_ * 4 + x_, y_ * 4 + zl_ * 2 + c_)

    right, left, across = at(x_=xp), at(x_=xm), at(zh_=oh)
    ways = (right, left)
    z_peers = (at(zl_=1 - zl), across, at(zh_=oh, zl_=1 - zl))
    y_peers = tuple(at(y_=lax.rem(y + d, 4)) for d in (1, 3, 2))
    twin = at(c_=1 - c)

    def send(src, dst, s, r, dev):
        return pltpu.make_async_remote_copy(src_ref=src, dst_ref=dst, send_sem=s, recv_sem=r, device_id=dev, device_id_type=MESH)


    def rows_of(i, plane):
        return pl.ds(pl.multiple_of((plane * nb + i) * R, R), R)

    def own(i, d):
        rows = rows_of(i, zh)
        return send(coef.at[rows], gath.at[x, zh, rows], own_s.at[d], own_r.at[d, i], ways[d])

    def partner(i, d):
        ref = gath.at[x, oh, rows_of(i, zh)]
        return send(ref, ref, par_s.at[d], par_r.at[d, i], ways[d])

    def forward(i, d):
        ref = gath.at[(xm, xp)[d], :, pl.ds(pl.multiple_of((zh * nb + i) * R + d * half, half), half)]
        return send(ref, ref, fwd_s.at[d], fwd_r.at[d, i], ways[d])

    def over(i):
        rows = rows_of(i, oh)
        return send(coef.at[rows], gath.at[x, zh, rows], k_s, k_r.at[i], across)

    def product(i):
        return send(prod.at[pl.ds(i * R, R)], out.at[rows_of(i, zh)], p_s, p_r, across)


    pair = (x, xm)
    feeder = (xm, xp)
    fed = (xp, x2)

    def pair_rows(i, j):
        return pl.ds(pl.multiple_of((2 * nb + j * nj + i) * R, R), R)

    def feed(i, d):
        rows = pair_rows(i, fed[d])
        return send(coef.at[rows], gath.at[x, zh, rows], feed_s.at[d], feed_r.at[d, i], ways[d])

    def pair_over(i, d):
        rows = pair_rows(i, pair[d])
        return send(coef.at[rows], gath.at[x, zh, rows], jk_s.at[d], jk_r.at[d, i], across)

    def feeder_over(i, d):
        ref = gath.at[feeder[d], zh, pair_rows(i, pair[d])]
        return send(ref, ref, jf_s.at[d], jf_r.at[d, i], across)

    def mate_own(i, d):
        ref = gath.at[x, :, pair_rows(i, pair[d])]
        return send(ref, ref, ma_s.at[d], ma_r.at[d, i], ways[d])

    def mate_fed(i, d):
        ref = gath.at[feeder[d], :, pair_rows(i, pair[d])]
        return send(ref, ref, mb_s.at[d], mb_r.at[d, i], ways[d])

    def pair_product(i, d):
        return send(jprod.at[d, pl.ds(i * R, R)], out.at[pair_rows(i, pair[d])], jo_s.at[d], jo_r.at[d], ways[1 - d])


    z_sends = [send(rot, full.at[(0, 1, 1)[k], y, zl, c], z_s.at[k], z_r.at[k], dev) for k, dev in enumerate(z_peers)]
    x_sends = [send(full.at[0, y, :, c], full.at[2 + d, y, :, c], x_s.at[d], x_r.at[d], ways[d]) for d in range(2)]

    def y_sends(g):
        ref = full.at[2 * g : 2 * g + 2, y, :, c]
        return [send(ref, ref, y_s.at[g, k], y_r.at[g, k], dev) for k, dev in enumerate(y_peers)]

    def c_send(g):
        ref = full.at[2 * g : 2 * g + 2, :, :, c]
        return send(ref, ref, c_s.at[g], c_r.at[g], twin)

    def times(rows, columns):
        lhs = jnp.concatenate([gath[b % 4, b // 4, rows, :] for b in range(8)], axis=1)
        rhs = full[columns].reshape(1024, full.shape[-1])
        return jnp.dot(lhs, rhs, preferred_element_type=jnp.float32).astype(out.dtype)

    local_rot = pltpu.make_async_copy(rot, full.at[0, y, zl, c], loc.at[0])
    local_coef = pltpu.make_async_copy(coef, gath.at[x, zh], loc.at[1])

    peers = (right, left, *z_peers, *y_peers, twin)
    barrier = pltpu.get_barrier_semaphore()
    for dev in peers:
        pl.semaphore_signal(barrier, inc=1, device_id=dev, device_id_type=MESH)
    local_rot.start()
    pl.semaphore_wait(barrier, len(peers))

    over(0).start()
    for i in range(OWN_AHEAD):
        for d in range(2):
            own(i, d).start()
    for s in z_sends:
        s.start()
    for i in range(1, K_AHEAD):
        over(i).start()
    local_coef.start()
    local_rot.wait()
    local_coef.wait()

    def begin(t):
        return jnp.maximum(0, jnp.minimum(jnp.minimum(2 * (t - START), t - L_MULTIPLY), nb))

    def between(t, first, count, step=1):
        inside = jnp.logical_and(t >= first, t < first + step * count)
        return inside if step == 1 else jnp.logical_and(inside, lax.rem(t - first + step, step) == 0)

    steps = max(nb + L_MULTIPLY, FIRST_PAIR + STRIDE * (nj - 1) + 1)

    @pl.loop(0, steps)
    def _(t):
        @pl.when(between(t, OWN_AHEAD, nb - OWN_AHEAD))
        def _():
            for d in range(2):
                own(t, d).start()

        @pl.when(between(t, 0, nb - K_AHEAD))
        def _():
            over(t + K_AHEAD).start()

        @pl.when(between(t, 0, nj))
        def _():
            for d in range(2):
                feed(t, d).start()
                pair_over(t, d).start()

        @pl.when(between(t, L_PARTNER, nb))
        def _():
            over(t - L_PARTNER).wait_recv()
            for d in range(2):
                partner(t - L_PARTNER, d).start()

        @pl.when(between(t, L_FEED, nj))
        def _():
            for d in range(2):
                feed(t - L_FEED, d).wait_recv()
                feeder_over(t - L_FEED, d).start()

        @pl.when(between(t, L_FORWARD, nb))
        def _():
            for d in range(2):
                own(t - L_FORWARD, d).wait_recv()
                partner(t - L_FORWARD, d).wait_recv()
                forward(t - L_FORWARD, d).start()

        @pl.when(between(t, FIRST_MATE, nj, STRIDE))
        def _():
            i = (t - FIRST_MATE) // STRIDE
            for d in range(2):
                pair_over(i, d).wait_recv()
                mate_own(i, d).start()
            for d in range(2):
                feeder_over(i, d).wait_recv()
                mate_fed(i, d).start()

        @pl.when(t == ROT_1)
        def _():
            for s in z_sends:
                s.wait()
            for s in x_sends:
                s.start()
            for s in y_sends(0):
                s.start()

        @pl.when(t == ROT_2)
        def _():
            for s in x_sends:
                s.wait()
            for s in y_sends(1):
                s.start()

        @pl.when(t == ROT_3)
        def _():
            for s in y_sends(0):
                s.wait()
            c_send(0).start()

        @pl.when(t == START)
        def _():
            c_send(0).wait()

        @pl.when(t == ROT_4)
        def _():
            for s in y_sends(1):
                s.wait()
            c_send(1).start()

        @pl.when(t == ROT_5)
        def _():
            c_send(1).wait()

        @pl.loop(begin(t), begin(t + 1))
        def _(i):
            for d in range(2):
                forward(i, d).wait_recv()
            rows = rows_of(i, zh)
            prod[pl.ds(i * R, R), :] = times(rows, 1)
            product(i).start()
            out[rows, :] = times(rows, 0)

        @pl.when(between(t, FIRST_PAIR, nj, STRIDE))
        def _():
            i = (t - FIRST_PAIR) // STRIDE
            for d in range(2):
                mate_own(i, 1 - d).wait_recv()
                mate_fed(i, 1 - d).wait_recv()
                rows = pair_rows(i, pair[d])
                jprod[d, pl.ds(i * R, R), :] = times(rows, 2 + d)
                pair_product(i, d).start()
            for d in range(2):
                rows = pair_rows(i, pair[d])
                out[rows, :] = times(rows, 0)


    send(prod, prod, p_s, p_r, across).wait()
    for d in range(2):
        send(jprod.at[d], jprod.at[d], jo_s.at[d], jo_r.at[d], ways[d]).wait()

    def sent(s, blocks):
        ref = gath.at[0, 0, pl.ds(0, blocks * R)]
        send(ref, ref, s, p_r, across).wait_send()

    sent(k_s, nb)
    for d in range(2):
        for s in (own_s, par_s, fwd_s):
            sent(s.at[d], nb)
        for s in (feed_s, jk_s, jf_s):
            sent(s.at[d], nj)
        for s in (ma_s, mb_s):
            sent(s.at[d], 2 * nj)


def on_device(coeffs, rotation):
    coeffs, rotation = (pltpu.with_memory_space_constraint(v, pltpu.HBM) for v in (coeffs, rotation))
    rows, depth = coeffs.shape
    columns = rotation.shape[1]
    nj = NJ
    nb = (rows // R - 4 * nj) // 2
    dma = pltpu.SemaphoreType.DMA
    dtype = coeffs.dtype
    return pl.pallas_call(
        functools.partial(kernel, nb, nj),
        out_shape=pltpu.VMEM((rows, columns), dtype),
        in_specs=[pl.BlockSpec(memory_space=pltpu.HBM)] * 2,
        out_specs=pl.BlockSpec(memory_space=pltpu.VMEM),
        scratch_shapes=[
            pltpu.VMEM((4, 2, rows, depth), dtype),
            pltpu.VMEM((4, 4, 2, 2, rotation.shape[0], columns), dtype),
            pltpu.VMEM((nb * R, columns), dtype),
            pltpu.VMEM((2, nj * R, columns), dtype),
            dma((2,)), dma((2, nb)), dma((2,)), dma((2, nb)), dma((2,)), dma((2, nb)), dma, dma((nb,)), dma, dma,
            dma((2,)), dma((2, nj)), dma((2,)), dma((2, nj)), dma((2,)), dma((2, nj)),
            dma((2,)), dma((2, nj)), dma((2,)), dma((2, nj)), dma((2,)), dma((2,)),
            dma((3,)), dma((3,)), dma((2,)), dma((2,)), dma((2, 3)), dma((2, 3)), dma((2,)), dma((2,)), dma((2,)),
        ],
        compiler_params=pltpu.CompilerParams(
            collective_id=0, has_side_effects=True, vmem_limit_bytes=40 * 2**20
        ),
        cost_estimate=pl.CostEstimate(flops=2 * rows * 1024 * columns, bytes_accessed=rows * columns * 2, transcendentals=0),
    )(coeffs, rotation)


def solution(mesh):
    return jax.shard_map(
        on_device,
        mesh=mesh,
        in_specs=(P("gvec", "band"), P("gvec", "band")),
        out_specs=P("gvec", "band"),
        check_vma=False,
    )
```

```python
import functools

import jax
import jax.numpy as jnp
from jax import lax
from jax.experimental import pallas as pl
from jax.experimental.pallas import tpu as pltpu
from jax.sharding import PartitionSpec as P

MESH = pl.DeviceIdType.MESH
R = 128
NJ, RJ = 6, 160
K_AHEAD, OWN_AHEAD = 2, 5
L_PARTNER, L_FORWARD, L_MULTIPLY = 3, 6, 10
L_FEED, FIRST_MATE, FIRST_PAIR, STRIDE = 5, 10, 16, 2
ROT_1, ROT_2, ROT_3, START, ROT_4, ROT_5 = 3, 7, 9, 11, 13, 14


def kernel(nb, nj, coef, rot, out, gath, full, prod, jprod, *sems):
    (own_s, own_r, par_s, par_r, fwd_s, fwd_r, k_s, k_r, p_s, p_r,
     feed_s, feed_r, jk_s, jk_r, jf_s, jf_r, ma_s, ma_r, mb_s, mb_r, jo_s, jo_r,
     z_s, z_r, x_s, x_r, y_s, y_r, c_s, c_r, loc) = sems
    half = R // 2
    band, gvec = lax.axis_index("band"), lax.axis_index("gvec")
    x, zh = lax.rem(band, 4), band // 4
    y, zl, c = gvec // 4, lax.rem(gvec // 2, 2), lax.rem(gvec, 2)
    xp, xm, x2 = lax.rem(x + 1, 4), lax.rem(x + 3, 4), lax.rem(x + 2, 4)
    oh = 1 - zh

    def at(x_=x, y_=y, zh_=zh, zl_=zl, c_=c):
        return (zh_ * 4 + x_, y_ * 4 + zl_ * 2 + c_)

    right, left, across = at(x_=xp), at(x_=xm), at(zh_=oh)
    ways = (right, left)
    z_peers = (at(zl_=1 - zl), across, at(zh_=oh, zl_=1 - zl))
    y_peers = tuple(at(y_=lax.rem(y + d, 4)) for d in (1, 3, 2))
    twin = at(c_=1 - c)

    def send(src, dst, s, r, dev):
        return pltpu.make_async_remote_copy(src_ref=src, dst_ref=dst, send_sem=s, recv_sem=r, device_id=dev, device_id_type=MESH)


    def rows_of(i, plane):
        return pl.ds(pl.multiple_of((plane * nb + i) * R, R), R)

    def own(i, d):
        rows = rows_of(i, zh)
        return send(coef.at[rows], gath.at[x, zh, rows], own_s.at[d], own_r.at[d, i], ways[d])

    def partner(i, d):
        ref = gath.at[x, oh, rows_of(i, zh)]
        return send(ref, ref, par_s.at[d], par_r.at[d, i], ways[d])

    def forward(i, d):
        ref = gath.at[(xm, xp)[d], :, pl.ds(pl.multiple_of((zh * nb + i) * R + d * half, half), half)]
        return send(ref, ref, fwd_s.at[d], fwd_r.at[d, i], ways[d])

    def over(i):
        rows = rows_of(i, oh)
        return send(coef.at[rows], gath.at[x, zh, rows], k_s, k_r.at[i], across)

    def product(i):
        return send(prod.at[pl.ds(i * R, R)], out.at[rows_of(i, zh)], p_s, p_r, across)


    pair = (x, xm)
    feeder = (xm, xp)
    fed = (xp, x2)

    def pair_rows(i, j):
        return pl.ds(pl.multiple_of(2 * nb * R + (j * nj + i) * RJ, 16), RJ)

    def feed(i, d):
        rows = pair_rows(i, fed[d])
        return send(coef.at[rows], gath.at[x, zh, rows], feed_s.at[d], feed_r.at[d, i], ways[d])

    def pair_over(i, d):
        rows = pair_rows(i, pair[d])
        return send(coef.at[rows], gath.at[x, zh, rows], jk_s.at[d], jk_r.at[d, i], across)

    def feeder_over(i, d):
        ref = gath.at[feeder[d], zh, pair_rows(i, pair[d])]
        return send(ref, ref, jf_s.at[d], jf_r.at[d, i], across)

    def mate_own(i, d):
        ref = gath.at[x, :, pair_rows(i, pair[d])]
        return send(ref, ref, ma_s.at[d], ma_r.at[d, i], ways[d])

    def mate_fed(i, d):
        ref = gath.at[feeder[d], :, pair_rows(i, pair[d])]
        return send(ref, ref, mb_s.at[d], mb_r.at[d, i], ways[d])

    def pair_product(i, d):
        return send(jprod.at[d, pl.ds(i * RJ, RJ)], out.at[pair_rows(i, pair[d])], jo_s.at[d], jo_r.at[d], ways[1 - d])


    z_sends = [send(rot, full.at[(0, 1, 1)[k], y, zl, c], z_s.at[k], z_r.at[k], dev) for k, dev in enumerate(z_peers)]
    x_sends = [send(full.at[0, y, :, c], full.at[2 + d, y, :, c], x_s.at[d], x_r.at[d], ways[d]) for d in range(2)]

    def y_sends(g):
        ref = full.at[2 * g : 2 * g + 2, y, :, c]
        return [send(ref, ref, y_s.at[g, k], y_r.at[g, k], dev) for k, dev in enumerate(y_peers)]

    def c_send(g):
        ref = full.at[2 * g : 2 * g + 2, :, :, c]
        return send(ref, ref, c_s.at[g], c_r.at[g], twin)

    def times(rows, columns):
        lhs = jnp.concatenate([gath[b % 4, b // 4, rows, :] for b in range(8)], axis=1)
        rhs = full[columns].reshape(1024, full.shape[-1])
        return jnp.dot(lhs, rhs, preferred_element_type=jnp.float32).astype(out.dtype)

    local_rot = pltpu.make_async_copy(rot, full.at[0, y, zl, c], loc.at[0])
    local_coef = pltpu.make_async_copy(coef, gath.at[x, zh], loc.at[1])

    peers = (right, left, *z_peers, *y_peers, twin)
    barrier = pltpu.get_barrier_semaphore()
    for dev in peers:
        pl.semaphore_signal(barrier, inc=1, device_id=dev, device_id_type=MESH)
    local_rot.start()
    pl.semaphore_wait(barrier, len(peers))

    over(0).start()
    for i in range(OWN_AHEAD):
        for d in range(2):
            own(i, d).start()
    for s in z_sends:
        s.start()
    for i in range(1, K_AHEAD):
        over(i).start()
    local_coef.start()
    local_rot.wait()
    local_coef.wait()

    def begin(t):
        return jnp.maximum(0, jnp.minimum(jnp.minimum(2 * (t - START), t - L_MULTIPLY), nb))

    def between(t, first, count, step=1):
        inside = jnp.logical_and(t >= first, t < first + step * count)
        return inside if step == 1 else jnp.logical_and(inside, lax.rem(t - first + step, step) == 0)

    steps = max(nb + L_MULTIPLY, FIRST_PAIR + STRIDE * (nj - 1) + 1)

    @pl.loop(0, steps)
    def _(t):
        @pl.when(between(t, OWN_AHEAD, nb - OWN_AHEAD))
        def _():
            for d in range(2):
                own(t, d).start()

        @pl.when(between(t, 0, nb - K_AHEAD))
        def _():
            over(t + K_AHEAD).start()

        @pl.when(between(t, 0, nj))
        def _():
            for d in range(2):
                feed(t, d).start()
                pair_over(t, d).start()

        @pl.when(between(t, L_PARTNER, nb))
        def _():
            over(t - L_PARTNER).wait_recv()
            for d in range(2):
                partner(t - L_PARTNER, d).start()

        @pl.when(between(t, L_FEED, nj))
        def _():
            for d in range(2):
                feed(t - L_FEED, d).wait_recv()
                feeder_over(t - L_FEED, d).start()

        @pl.when(between(t, L_FORWARD, nb))
        def _():
            for d in range(2):
                own(t - L_FORWARD, d).wait_recv()
                partner(t - L_FORWARD, d).wait_recv()
                forward(t - L_FORWARD, d).start()

        @pl.when(between(t, FIRST_MATE, nj, STRIDE))
        def _():
            i = (t - FIRST_MATE) // STRIDE
            for d in range(2):
                pair_over(i, d).wait_recv()
                mate_own(i, d).start()
            for d in range(2):
                feeder_over(i, d).wait_recv()
                mate_fed(i, d).start()

        @pl.when(t == ROT_1)
        def _():
            for s in z_sends:
                s.wait()
            for s in x_sends:
                s.start()
            for s in y_sends(0):
                s.start()

        @pl.when(t == ROT_2)
        def _():
            for s in x_sends:
                s.wait()
            for s in y_sends(1):
                s.start()

        @pl.when(t == ROT_3)
        def _():
            for s in y_sends(0):
                s.wait()
            c_send(0).start()

        @pl.when(t == START)
        def _():
            c_send(0).wait()

        @pl.when(t == ROT_4)
        def _():
            for s in y_sends(1):
                s.wait()
            c_send(1).start()

        @pl.when(t == ROT_5)
        def _():
            c_send(1).wait()

        @pl.loop(begin(t), begin(t + 1))
        def _(i):
            for d in range(2):
                forward(i, d).wait_recv()
            rows = rows_of(i, zh)
            prod[pl.ds(i * R, R), :] = times(rows, 1)
            product(i).start()
            out[rows, :] = times(rows, 0)

        @pl.when(between(t, FIRST_PAIR, nj, STRIDE))
        def _():
            i = (t - FIRST_PAIR) // STRIDE
            for d in range(2):
                mate_own(i, 1 - d).wait_recv()
                mate_fed(i, 1 - d).wait_recv()
                rows = pair_rows(i, pair[d])
                jprod[d, pl.ds(i * RJ, RJ), :] = times(rows, 2 + d)
                pair_product(i, d).start()
            for d in range(2):
                rows = pair_rows(i, pair[d])
                out[rows, :] = times(rows, 0)


    send(prod, prod, p_s, p_r, across).wait()
    for d in range(2):
        send(jprod.at[d], jprod.at[d], jo_s.at[d], jo_r.at[d], ways[d]).wait()

    def sent(s, rows):
        ref = gath.at[0, 0, pl.ds(0, rows)]
        send(ref, ref, s, p_r, across).wait_send()

    sent(k_s, nb * R)
    for d in range(2):
        for s in (own_s, par_s, fwd_s):
            sent(s.at[d], nb * R)
        for s in (feed_s, jk_s, jf_s):
            sent(s.at[d], nj * RJ)
        for s in (ma_s, mb_s):
            sent(s.at[d], 2 * nj * RJ)


def on_device(coeffs, rotation):
    coeffs, rotation = (pltpu.with_memory_space_constraint(v, pltpu.HBM) for v in (coeffs, rotation))
    rows, depth = coeffs.shape
    columns = rotation.shape[1]
    nj = NJ
    nb = (rows - 4 * nj * RJ) // (2 * R)
    dma = pltpu.SemaphoreType.DMA
    dtype = coeffs.dtype
    return pl.pallas_call(
        functools.partial(kernel, nb, nj),
        out_shape=pltpu.VMEM((rows, columns), dtype),
        in_specs=[pl.BlockSpec(memory_space=pltpu.HBM)] * 2,
        out_specs=pl.BlockSpec(memory_space=pltpu.VMEM),
        scratch_shapes=[
            pltpu.VMEM((4, 2, rows, depth), dtype),
            pltpu.VMEM((4, 4, 2, 2, rotation.shape[0], columns), dtype),
            pltpu.VMEM((nb * R, columns), dtype),
            pltpu.VMEM((2, nj * RJ, columns), dtype),
            dma((2,)), dma((2, nb)), dma((2,)), dma((2, nb)), dma((2,)), dma((2, nb)), dma, dma((nb,)), dma, dma,
            dma((2,)), dma((2, nj)), dma((2,)), dma((2, nj)), dma((2,)), dma((2, nj)),
            dma((2,)), dma((2, nj)), dma((2,)), dma((2, nj)), dma((2,)), dma((2,)),
            dma((3,)), dma((3,)), dma((2,)), dma((2,)), dma((2, 3)), dma((2, 3)), dma((2,)), dma((2,)), dma((2,)),
        ],
        compiler_params=pltpu.CompilerParams(
            collective_id=0, has_side_effects=True, vmem_limit_bytes=40 * 2**20
        ),
        cost_estimate=pl.CostEstimate(flops=2 * rows * 1024 * columns, bytes_accessed=rows * columns * 2, transcendentals=0),
    )(coeffs, rotation)


def solution(mesh):
    return jax.shard_map(
        on_device,
        mesh=mesh,
        in_specs=(P("gvec", "band"), P("gvec", "band")),
        out_specs=P("gvec", "band"),
        check_vma=False,
    )
```

```python
import functools

import jax
import jax.numpy as jnp
from jax import lax
from jax.experimental import pallas as pl
from jax.experimental.pallas import tpu as pltpu
from jax.sharding import PartitionSpec as P

MESH = pl.DeviceIdType.MESH
R = 128
NJ, RJ = 6, 160
K_AHEAD, OWN_AHEAD = 2, 5
L_PARTNER, L_FORWARD, L_MULTIPLY = 3, 6, 10
L_FEED, FIRST_MATE, FIRST_PAIR, STRIDE = 5, 10, 15, 2
ROT_1, ROT_2, ROT_3, START, ROT_4, ROT_5 = 3, 7, 9, 11, 13, 14


def kernel(nb, nj, coef, rot, out, gath, full, prod, jprod, *sems):
    (own_s, own_r, par_s, par_r, fwd_s, fwd_r, k_s, k_r, p_s, p_r,
     feed_s, feed_r, jk_s, jk_r, jf_s, jf_r, ma_s, ma_r, mb_s, mb_r, jo_s, jo_r,
     z_s, z_r, x_s, x_r, y_s, y_r, c_s, c_r, loc) = sems
    half = R // 2
    band, gvec = lax.axis_index("band"), lax.axis_index("gvec")
    x, zh = lax.rem(band, 4), band // 4
    y, zl, c = gvec // 4, lax.rem(gvec // 2, 2), lax.rem(gvec, 2)
    xp, xm, x2 = lax.rem(x + 1, 4), lax.rem(x + 3, 4), lax.rem(x + 2, 4)
    oh = 1 - zh

    def at(x_=x, y_=y, zh_=zh, zl_=zl, c_=c):
        return (zh_ * 4 + x_, y_ * 4 + zl_ * 2 + c_)

    right, left, across = at(x_=xp), at(x_=xm), at(zh_=oh)
    ways = (right, left)
    z_peers = (at(zl_=1 - zl), across, at(zh_=oh, zl_=1 - zl))
    y_peers = tuple(at(y_=lax.rem(y + d, 4)) for d in (1, 3, 2))
    twin = at(c_=1 - c)

    def send(src, dst, s, r, dev):
        return pltpu.make_async_remote_copy(src_ref=src, dst_ref=dst, send_sem=s, recv_sem=r, device_id=dev, device_id_type=MESH)


    def rows_of(i, plane):
        return pl.ds(pl.multiple_of((plane * nb + i) * R, R), R)

    def own(i, d):
        rows = rows_of(i, zh)
        return send(coef.at[rows], gath.at[x, zh, rows], own_s.at[d], own_r.at[d, i], ways[d])

    def partner(i, d):
        ref = gath.at[x, oh, rows_of(i, zh)]
        return send(ref, ref, par_s.at[d], par_r.at[d, i], ways[d])

    def forward(i, d):
        ref = gath.at[(xm, xp)[d], :, pl.ds(pl.multiple_of((zh * nb + i) * R + d * half, half), half)]
        return send(ref, ref, fwd_s.at[d], fwd_r.at[d, i], ways[d])

    def over(i):
        rows = rows_of(i, oh)
        return send(coef.at[rows], gath.at[x, zh, rows], k_s, k_r.at[i], across)

    def product(i):
        return send(prod.at[pl.ds(i * R, R)], out.at[rows_of(i, zh)], p_s, p_r, across)


    pair = (x, xm)
    feeder = (xm, xp)
    fed = (xp, x2)

    def pair_rows(i, j):
        return pl.ds(pl.multiple_of(2 * nb * R + (j * nj + i) * RJ, 16), RJ)

    def feed(i, d):
        rows = pair_rows(i, fed[d])
        return send(coef.at[rows], gath.at[x, zh, rows], feed_s.at[d], feed_r.at[d, i], ways[d])

    def pair_over(i, d):
        rows = pair_rows(i, pair[d])
        return send(coef.at[rows], gath.at[x, zh, rows], jk_s.at[d], jk_r.at[d, i], across)

    def feeder_over(i, d):
        ref = gath.at[feeder[d], zh, pair_rows(i, pair[d])]
        return send(ref, ref, jf_s.at[d], jf_r.at[d, i], across)

    def mate_own(i, d):
        ref = gath.at[x, :, pair_rows(i, pair[d])]
        return send(ref, ref, ma_s.at[d], ma_r.at[d, i], ways[d])

    def mate_fed(i, d):
        ref = gath.at[feeder[d], :, pair_rows(i, pair[d])]
        return send(ref, ref, mb_s.at[d], mb_r.at[d, i], ways[d])

    def pair_product(i, d):
        return send(jprod.at[d, pl.ds(i * RJ, RJ)], out.at[pair_rows(i, pair[d])], jo_s.at[d], jo_r.at[d], ways[1 - d])


    z_sends = [send(rot, full.at[(0, 1, 1)[k], y, zl, c], z_s.at[k], z_r.at[k], dev) for k, dev in enumerate(z_peers)]
    x_sends = [send(full.at[0, y, :, c], full.at[2 + d, y, :, c], x_s.at[d], x_r.at[d], ways[d]) for d in range(2)]

    def y_sends(g):
        ref = full.at[2 * g : 2 * g + 2, y, :, c]
        return [send(ref, ref, y_s.at[g, k], y_r.at[g, k], dev) for k, dev in enumerate(y_peers)]

    def c_send(g):
        ref = full.at[2 * g : 2 * g + 2, :, :, c]
        return send(ref, ref, c_s.at[g], c_r.at[g], twin)

    def times(rows, columns):
        lhs = jnp.concatenate([gath[b % 4, b // 4, rows, :] for b in range(8)], axis=1)
        rhs = full[columns].reshape(1024, full.shape[-1])
        return jnp.dot(lhs, rhs, preferred_element_type=jnp.float32).astype(out.dtype)

    local_rot = pltpu.make_async_copy(rot, full.at[0, y, zl, c], loc.at[0])
    local_coef = pltpu.make_async_copy(coef, gath.at[x, zh], loc.at[1])

    peers = (right, left, *z_peers, *y_peers, twin)
    barrier = pltpu.get_barrier_semaphore()
    for dev in peers:
        pl.semaphore_signal(barrier, inc=1, device_id=dev, device_id_type=MESH)
    local_rot.start()
    pl.semaphore_wait(barrier, len(peers))

    over(0).start()
    for i in range(OWN_AHEAD):
        for d in range(2):
            own(i, d).start()
    for s in z_sends:
        s.start()
    for i in range(1, K_AHEAD):
        over(i).start()
    local_coef.start()
    local_rot.wait()
    local_coef.wait()

    def begin(t):
        return jnp.maximum(0, jnp.minimum(jnp.minimum(2 * (t - START), t - L_MULTIPLY), nb))

    def between(t, first, count, step=1):
        inside = jnp.logical_and(t >= first, t < first + step * count)
        return inside if step == 1 else jnp.logical_and(inside, lax.rem(t - first + step, step) == 0)

    steps = max(nb + L_MULTIPLY, FIRST_PAIR + STRIDE * (nj - 1) + 1)

    @pl.loop(0, steps)
    def _(t):
        @pl.when(between(t, OWN_AHEAD, nb - OWN_AHEAD))
        def _():
            for d in range(2):
                own(t, d).start()

        @pl.when(between(t, 0, nb - K_AHEAD))
        def _():
            over(t + K_AHEAD).start()

        @pl.when(between(t, 0, nj))
        def _():
            for d in range(2):
                feed(t, d).start()
                pair_over(t, d).start()

        @pl.when(between(t, L_PARTNER, nb))
        def _():
            over(t - L_PARTNER).wait_recv()
            for d in range(2):
                partner(t - L_PARTNER, d).start()

        @pl.when(between(t, L_FEED, nj))
        def _():
            for d in range(2):
                feed(t - L_FEED, d).wait_recv()
                feeder_over(t - L_FEED, d).start()

        @pl.when(between(t, L_FORWARD, nb))
        def _():
            for d in range(2):
                own(t - L_FORWARD, d).wait_recv()
                partner(t - L_FORWARD, d).wait_recv()
                forward(t - L_FORWARD, d).start()

        @pl.when(between(t, FIRST_MATE, nj, STRIDE))
        def _():
            i = (t - FIRST_MATE) // STRIDE
            for d in range(2):
                pair_over(i, d).wait_recv()
                mate_own(i, d).start()
            for d in range(2):
                feeder_over(i, d).wait_recv()
                mate_fed(i, d).start()

        @pl.when(t == ROT_1)
        def _():
            for s in z_sends:
                s.wait()
            for s in x_sends:
                s.start()
            for s in y_sends(0):
                s.start()

        @pl.when(t == ROT_2)
        def _():
            for s in x_sends:
                s.wait()
            for s in y_sends(1):
                s.start()

        @pl.when(t == ROT_3)
        def _():
            for s in y_sends(0):
                s.wait()
            c_send(0).start()

        @pl.when(t == START)
        def _():
            c_send(0).wait()

        @pl.when(t == ROT_4)
        def _():
            for s in y_sends(1):
                s.wait()
            c_send(1).start()

        @pl.when(t == ROT_5)
        def _():
            c_send(1).wait()

        @pl.loop(begin(t), begin(t + 1))
        def _(i):
            for d in range(2):
                forward(i, d).wait_recv()
            rows = rows_of(i, zh)
            prod[pl.ds(i * R, R), :] = times(rows, 1)
            product(i).start()
            out[rows, :] = times(rows, 0)

        @pl.when(between(t, FIRST_PAIR, nj, STRIDE))
        def _():
            i = (t - FIRST_PAIR) // STRIDE
            for d in range(2):
                mate_own(i, 1 - d).wait_recv()
                mate_fed(i, 1 - d).wait_recv()
                rows = pair_rows(i, pair[d])
                jprod[d, pl.ds(i * RJ, RJ), :] = times(rows, 2 + d)
                pair_product(i, d).start()
            for d in range(2):
                rows = pair_rows(i, pair[d])
                out[rows, :] = times(rows, 0)


    send(prod, prod, p_s, p_r, across).wait()
    for d in range(2):
        send(jprod.at[d], jprod.at[d], jo_s.at[d], jo_r.at[d], ways[d]).wait()

    def sent(s, rows):
        ref = gath.at[0, 0, pl.ds(0, rows)]
        send(ref, ref, s, p_r, across).wait_send()

    sent(k_s, nb * R)
    for d in range(2):
        for s in (own_s, par_s, fwd_s):
            sent(s.at[d], nb * R)
        for s in (feed_s, jk_s, jf_s):
            sent(s.at[d], nj * RJ)
        for s in (ma_s, mb_s):
            sent(s.at[d], 2 * nj * RJ)


def on_device(coeffs, rotation):
    coeffs, rotation = (pltpu.with_memory_space_constraint(v, pltpu.HBM) for v in (coeffs, rotation))
    rows, depth = coeffs.shape
    columns = rotation.shape[1]
    nj = NJ
    nb = (rows - 4 * nj * RJ) // (2 * R)
    dma = pltpu.SemaphoreType.DMA
    dtype = coeffs.dtype
    return pl.pallas_call(
        functools.partial(kernel, nb, nj),
        out_shape=pltpu.VMEM((rows, columns), dtype),
        in_specs=[pl.BlockSpec(memory_space=pltpu.HBM)] * 2,
        out_specs=pl.BlockSpec(memory_space=pltpu.VMEM),
        scratch_shapes=[
            pltpu.VMEM((4, 2, rows, depth), dtype),
            pltpu.VMEM((4, 4, 2, 2, rotation.shape[0], columns), dtype),
            pltpu.VMEM((nb * R, columns), dtype),
            pltpu.VMEM((2, nj * RJ, columns), dtype),
            dma((2,)), dma((2, nb)), dma((2,)), dma((2, nb)), dma((2,)), dma((2, nb)), dma, dma((nb,)), dma, dma,
            dma((2,)), dma((2, nj)), dma((2,)), dma((2, nj)), dma((2,)), dma((2, nj)),
            dma((2,)), dma((2, nj)), dma((2,)), dma((2, nj)), dma((2,)), dma((2,)),
            dma((3,)), dma((3,)), dma((2,)), dma((2,)), dma((2, 3)), dma((2, 3)), dma((2,)), dma((2,)), dma((2,)),
        ],
        compiler_params=pltpu.CompilerParams(
            collective_id=0, has_side_effects=True, vmem_limit_bytes=40 * 2**20
        ),
        cost_estimate=pl.CostEstimate(flops=2 * rows * 1024 * columns, bytes_accessed=rows * columns * 2, transcendentals=0),
    )(coeffs, rotation)


def solution(mesh):
    return jax.shard_map(
        on_device,
        mesh=mesh,
        in_specs=(P("gvec", "band"), P("gvec", "band")),
        out_specs=P("gvec", "band"),
        check_vma=False,
    )
```
